512 devices in a mesh: rep: 32 (over y_lo, z, core), fsdp: 16 (over y_hi, x).
Axes of the slice: x: 4, y: 8 (y_hi: 4, y_lo: 2; y = y_hi * 2 + y_lo), z: 8, core: 2. Of those that a mesh axis runs over, the one named last changes fastest.
Arguments:
- tokens: bfloat16 [98304, 2048], P(('rep', 'fsdp')), may hold values from -6 to 6
- weight: bfloat16 [65536, 2048], P(('rep', 'fsdp')), may hold values from -6 to 6
- gain: bfloat16 [65536], P(('rep', 'fsdp')), may hold values from 0.5 to 1.5
- upstream: bfloat16 [98304, 2048], P(('rep', 'fsdp')), may hold values from -6 to 6
- step: int32 [1], replicated, may hold values from 0 to 63
Outputs:
- projected: bfloat16 [98304, 2048], P(('rep', 'fsdp'))
- input_gradient: bfloat16 [98304, 2048], P(('rep', 'fsdp'))
- new_weight: bfloat16 [65536, 2048], P(('rep', 'fsdp'))
- new_gain: bfloat16 [65536], P(('rep', 'fsdp'))
The draws below stay inside these ranges and needn't reach their ends.
All inputs are finite; a program needn't handle non-finite values.
Results may differ from the reference program's by a relative error of at most 0.0058.
Values may be sent and summed in bfloat16 or wider, within the bound.
No kernel may reach another device: no remote copies, remote signals or barrier semaphores. Data moves between devices by JAX's collectives and lax.ppermute only.
A program may use at most 128 MiB of HBM per device.

```python
import math
import jax
import jax.numpy as jnp
from jax import lax

INPUT_FEATURES = 2048
F = 2048
DEVICE_TOKENS = 192
TOKENS = 98304
ROWS = 65536
N_REP = 32
N_FSDP = 16


def level_of(key, shape, split, least, high):
    def one(position, shards_of):
        draws = jax.random.uniform(jax.random.fold_in(jax.random.fold_in(key, 6), position), (shards_of,), jnp.float32, least / len(split), high / len(split))
        return jnp.repeat(jnp.exp(draws), shape[position] // shards_of).reshape((-1,) + (1,) * (len(shape) - position - 1))

    level = one(*split[0])
    for cut in split[1:]:
        level = level * one(*cut)
    return level


def noise(rng, dims, width, reach, split=(), dtype=jnp.bfloat16):
    factor_of = level_of(rng, dims, split, -0.22, 0.18) if split else 1.0
    drawn = jax.random.normal(rng, dims, jnp.float32) * width * factor_of
    return jnp.minimum(jnp.maximum(drawn, -reach), reach).astype(dtype)


def setup_inputs(seed: int = 0) -> dict:
    keys = jax.random.split(jax.random.key(seed), 6)
    tokens = noise(keys[0], (TOKENS, INPUT_FEATURES), 1.0, 6.0, ((0, 512),))
    weight = noise(keys[1], (ROWS, F), 1.0, 6.0, ((0, 512),))
    gain = jnp.clip(1.0 + 0.1 * jax.random.normal(keys[2], (ROWS,), jnp.float32), 0.5, 1.5).astype(jnp.bfloat16)
    upstream = noise(keys[3], (TOKENS, F), 1.0, 6.0, ((0, 512),))
    step = jax.random.randint(keys[4], (1,), 0, 64).astype(jnp.int32)
    return {"tokens": tokens, "weight": weight, "gain": gain, "upstream": upstream, "step": step}


eps = 1e-05
step_rate = 0.75
gain_rate = 0.004

def group_pass(items):
    inputs, weight, gain, upstream = items
    scale = 1.0 / math.sqrt(INPUT_FEATURES)
    input_float = inputs.astype(jnp.float32)
    inverse_deviation = lax.rsqrt(lax.optimization_barrier(jnp.mean(input_float * input_float, axis=1, keepdims=True)) + eps)
    normalized_input = input_float * inverse_deviation
    gain_float = gain.astype(jnp.float32)
    normed_rows = (normalized_input * gain_float).astype(jnp.bfloat16)
    projected = (jnp.dot(normed_rows, weight, preferred_element_type=jnp.float32) * scale).astype(jnp.bfloat16)
    normed_gradient = lax.dot_general(upstream, weight, (((1,), (1,)), ((), ())), preferred_element_type=jnp.float32) * scale
    scaled_rows = gain_float * normed_gradient
    input_gradient = (inverse_deviation * (scaled_rows - normalized_input * lax.optimization_barrier(jnp.mean(scaled_rows * normalized_input, axis=1, keepdims=True)))).astype(jnp.bfloat16)
    blocks_n = normed_rows.reshape(N_FSDP, DEVICE_TOKENS, INPUT_FEATURES)
    blocks_u = upstream.reshape(N_FSDP, DEVICE_TOKENS, F)
    gain_blocks = (normed_gradient * normalized_input).reshape(N_FSDP, DEVICE_TOKENS, INPUT_FEATURES)

    def accumulate(carry, block):
        left, right, prod = block
        part_w = (lax.dot_general(left, right, (((0,), (0,)), ((), ())), preferred_element_type=jnp.float32) * scale).astype(jnp.bfloat16)
        gain_portion = lax.optimization_barrier(jnp.sum(prod, axis=0)).astype(jnp.bfloat16)
        return ((carry[0] + part_w.astype(jnp.float32), carry[1] + gain_portion.astype(jnp.float32)), 0)
    init = (jnp.zeros((INPUT_FEATURES, F), jnp.float32), jnp.zeros((INPUT_FEATURES,), jnp.float32))
    (grad_w, grad_g), unused = lax.scan(accumulate, init, (blocks_n, blocks_u, gain_blocks))
    stepped_w = (weight.astype(jnp.float32) - step_rate * grad_w).astype(jnp.bfloat16)
    stepped_g = (gain_float - gain_rate * grad_g).astype(jnp.bfloat16)
    return (projected, input_gradient, stepped_w, stepped_g)

def reference(tokens, weight, gain, upstream, step):
    groups = N_REP
    projected, input_gradient, stepped_w, stepped_g = lax.map(group_pass, (tokens.reshape(groups, N_FSDP * DEVICE_TOKENS, INPUT_FEATURES), weight.reshape(groups, INPUT_FEATURES, F), gain.reshape(groups, INPUT_FEATURES), upstream.reshape(groups, N_FSDP * DEVICE_TOKENS, F)))
    hop = jnp.left_shift(jnp.int32(1), step[0] % 4)
    peer_w = jnp.roll(stepped_w, hop, axis=0)
    peer_g = jnp.roll(stepped_g, hop, axis=0)
    new_weight = (0.5 * (stepped_w.astype(jnp.float32) + peer_w.astype(jnp.float32))).astype(jnp.bfloat16)
    new_gain = (0.5 * (stepped_g.astype(jnp.float32) + peer_g.astype(jnp.float32))).astype(jnp.bfloat16)
    return (projected.reshape(groups * N_FSDP * DEVICE_TOKENS, F), input_gradient.reshape(groups * N_FSDP * DEVICE_TOKENS, INPUT_FEATURES), new_weight.reshape(groups * INPUT_FEATURES, F), new_gain.reshape(groups * INPUT_FEATURES))
```

```python
import math

import jax
import jax.numpy as jnp
from jax import lax
from jax.sharding import Mesh
from jax.sharding import PartitionSpec as P

eps = 1e-05
step_rate = 0.75
gain_rate = 0.004
F32 = jnp.float32
BF16 = jnp.bfloat16


def shifted(value, axis, steps):
    count = lax.axis_size(axis)
    pairs = [(source, (source + steps) % count) for source in range(count)]
    return lax.ppermute(value, axis, pairs)


def gossip_branch(distance):
    def branch(params):
        return jax.tree.map(lambda part: shifted(part, "rep", distance), params)

    return branch


def exchange(blocks, axis):
    return lax.all_to_all(blocks, axis, split_axis=0, concat_axis=0, tiled=True)


def on_device(tokens, weight, gain, upstream, step):
    n_x, n_y = lax.axis_size("x"), lax.axis_size("yh")
    rows, width_out = weight.shape
    count, width_in = tokens.shape
    scale = 1.0 / math.sqrt(width_in)
    me = lax.axis_index("x")

    offsets = (1, n_x - 1, 2)
    arrived = [shifted(upstream, "x", d) for d in offsets]
    full_weight = lax.all_gather(weight, "yh", axis=0, tiled=True)
    full_gain = lax.all_gather(gain, "yh", axis=0, tiled=True).astype(F32)

    input_float = tokens.astype(F32)
    inverse_deviation = lax.rsqrt(jnp.mean(input_float * input_float, axis=1, keepdims=True) + eps)
    normalized_input = input_float * inverse_deviation
    sent = normalized_input.astype(BF16).reshape(count, n_y, n_x, rows)
    sent = sent.transpose(2, 0, 1, 3).reshape(n_x, count, n_y * rows)
    xhat = exchange(sent, "x").reshape(n_x * count, n_y * rows).astype(F32)
    normed_rows = (xhat * full_gain).astype(BF16)

    gathered = jnp.zeros((n_x, count, width_out), BF16)
    gathered = lax.dynamic_update_slice(gathered, upstream[None], (me, 0, 0))
    for d, block in zip(offsets, arrived):
        gathered = lax.dynamic_update_slice(gathered, block[None], ((me + n_x - d) % n_x, 0, 0))
    gathered = gathered.reshape(n_x * count, width_out)

    part_w = (
        lax.dot_general(normed_rows, gathered, (((0,), (0,)), ((), ())), preferred_element_type=F32)
        * scale
    ).astype(BF16)
    grad_w = lax.psum_scatter(part_w, "yh", scatter_dimension=0, tiled=True).astype(F32)
    stepped_w = (weight.astype(F32) - step_rate * grad_w).astype(BF16)

    part_p = (jnp.dot(normed_rows, full_weight, preferred_element_type=F32) * scale).astype(BF16)
    normed_gradient = (
        lax.dot_general(gathered, full_weight, (((1,), (1,)), ((), ())), preferred_element_type=F32)
        * scale
    )
    part_g = jnp.sum(normed_gradient * xhat, axis=0).astype(BF16)
    scaled = (full_gain * normed_gradient).astype(BF16).reshape(n_x, count, n_y * rows)
    scaled_back = exchange(scaled, "x")
    pieces_p = exchange(part_p.reshape(n_x, count, width_out), "x")
    pieces_g = exchange(part_g.reshape(n_y, rows), "yh")

    projected = jnp.sum(pieces_p.astype(F32), axis=0).astype(BF16)
    scaled_rows = scaled_back.reshape(n_x, count, n_y, rows).transpose(1, 2, 0, 3)
    scaled_rows = scaled_rows.reshape(count, width_in).astype(F32)
    input_gradient = (
        inverse_deviation
        * (
            scaled_rows
            - normalized_input * jnp.mean(scaled_rows * normalized_input, axis=1, keepdims=True)
        )
    ).astype(BF16)
    grad_g = jnp.sum(pieces_g.astype(F32), axis=0)
    stepped_g = (gain.astype(F32) - gain_rate * grad_g).astype(BF16)

    branches = [gossip_branch(distance) for distance in (1, 2, 4, 8)]
    peer_w, peer_g = lax.switch(step[0] % 4, branches, (stepped_w, stepped_g))
    new_weight = (0.5 * (stepped_w.astype(F32) + peer_w.astype(F32))).astype(BF16)
    new_gain = (0.5 * (stepped_g.astype(F32) + peer_g.astype(F32))).astype(BF16)
    return (projected, input_gradient, new_weight, new_gain)


def solution(mesh):
    n_rep, n_fsdp = mesh.devices.shape
    n_x = 4
    split = Mesh(mesh.devices.reshape(n_rep, n_fsdp // n_x, n_x), ("rep", "yh", "x"))
    every = ("rep", "yh", "x")
    placed = (P(every, None), P(every, None), P(every), P(every, None), P())
    return jax.shard_map(
        on_device,
        mesh=split,
        in_specs=placed,
        out_specs=(P(every, None), P(every, None), P(every, None), P(every)),
        check_vma=False,
    )
```

```python
import functools
import math

import jax
import jax.numpy as jnp
from jax import lax
from jax.experimental import pallas as pl
from jax.experimental.pallas import tpu as pltpu
from jax.sharding import Mesh
from jax.sharding import PartitionSpec as P

eps = 1e-05
step_rate = 0.75
gain_rate = 0.004
F32 = jnp.float32
BF16 = jnp.bfloat16
VMEM_LIMIT = 32 * 1024 * 1024
ANY = pl.BlockSpec(memory_space=pl.ANY)
BLOCK = None
SCALAR = pl.BlockSpec(memory_space=pltpu.SMEM)


def array(shape, dtype=BF16):
    return jax.ShapeDtypeStruct(shape, dtype)


def in_hbm(shape, dtype=BF16):
    return pltpu.HBM(shape, dtype)


def call(kernel, ins, outs, scratch=(), flops=0, moved=0):
    values = [
        v if spec is SCALAR else pltpu.with_memory_space_constraint(v, pltpu.HBM) for v, spec in ins
    ]
    return pl.pallas_call(
        kernel,
        grid=(1,),
        out_shape=list(outs),
        in_specs=[whole(v.shape) if spec is BLOCK else spec for v, spec in ins],
        out_specs=[whole(shape.shape) for shape in outs],
        scratch_shapes=list(scratch),
        compiler_params=pltpu.CompilerParams(vmem_limit_bytes=VMEM_LIMIT),
        cost_estimate=pl.CostEstimate(flops=flops, bytes_accessed=moved, transcendentals=0),
    )(*values)


def whole(shape):
    return pl.BlockSpec(shape, lambda s: (0,) * len(shape))


def fetch(pairs, sems):
    copies = [pltpu.make_async_copy(src, dst, sems.at[i]) for i, (src, dst) in enumerate(pairs)]
    for copy in copies:
        copy.start()
    return copies


def shifted(value, axis, steps):
    count = lax.axis_size(axis)
    pairs = [(source, (source + steps) % count) for source in range(count)]
    return lax.ppermute(value, axis, pairs)


def exchange(blocks, axis):
    return lax.all_to_all(blocks, axis, split_axis=0, concat_axis=0, tiled=True)


def column_of(row):
    n = row.shape[1]
    down = lax.broadcasted_iota(jnp.int32, (n, n), 0)
    along = lax.broadcasted_iota(jnp.int32, (n, n), 1)
    return jnp.sum(jnp.where(down == along, row, 0.0), axis=1, keepdims=True)


def row_of(column):
    n = column.shape[0]
    down = lax.broadcasted_iota(jnp.int32, (n, n), 0)
    along = lax.broadcasted_iota(jnp.int32, (n, n), 1)
    return jnp.sum(jnp.where(down == along, column, 0.0), axis=0, keepdims=True)


def weight_kernel(weight_ref, gain_ref, out_ref):
    scaled = (weight_ref[...].astype(F32) * column_of(gain_ref[...].astype(F32))).astype(BF16)
    for i in range(out_ref.shape[0]):
        out_ref[i] = scaled


def token_kernel(
    n_x, me_ref, tok_ref, up_ref, dep_ref, own_ref, sa_ref, sb_ref, ta_ref, tb_ref, rstd_ref
):
    me = me_ref[0]
    width, part = tok_ref.shape[1], own_ref.shape[1]
    rows = part // (width // part)
    half, quarter = width // 2, part // 2
    for d in range(n_x):
        slot = lax.rem(me + d, n_x) * rows
        for k in range(part // rows):
            block = tok_ref[:, pl.ds(pl.multiple_of(slot + k * n_x * rows, rows), rows)]
            at = k * rows
            if d == 0:
                own_ref[:, at : at + rows] = block
            elif d == 1:
                ta_ref[:, half + at : half + at + rows] = block
            elif d == 3:
                tb_ref[:, half + at : half + at + rows] = block
            elif at < quarter:
                sa_ref[:, half + at : half + at + rows] = block
            else:
                sb_ref[:, half + at - quarter : half + at - quarter + rows] = block
    x = tok_ref[...].astype(F32)
    rstd = lax.rsqrt(jnp.mean(x * x, axis=1, keepdims=True) + eps)
    rstd_ref[...] = jnp.broadcast_to(rstd, rstd_ref.shape)
    up_a = (up_ref[:, :half].astype(F32) * rstd).astype(BF16)
    up_b = (up_ref[:, half:].astype(F32) * rstd).astype(BF16)
    sa_ref[:, :half] = up_a
    tb_ref[:, :half] = up_a
    sb_ref[:, :half] = up_b
    ta_ref[:, :half] = up_b


def grad_kernel(scale, xo, lt, rt, fa, fb, sa, la, sb, rb, out, *scratch):
    (vx, vlt, vrt, vfa, vfb, vsa, vla, vsb, vrb), turned, sems = scratch[:9], scratch[9], scratch[10]
    half = vsa.shape[1]
    rows = out.shape[1]
    tile = 256
    copies = fetch(
        [
            (xo, vx),
            (lt, vlt),
            (rt, vrt),
            (fa, vfa),
            (fb, vfb),
            (sa.at[:, :half], vsa),
            (la.at[:, :half], vla),
            (sb.at[:, :half], vsb),
            (rb.at[:, :half], vrb),
        ],
        sems,
    )
    for copy in copies[:5]:
        copy.wait()
    far = jnp.concatenate([vfa[:, half:], vfb[:, half:]], axis=1)
    turned[...] = jnp.concatenate([vx[...], vlt[:, half:], vrt[:, half:], far], axis=0).T
    for h, refs in enumerate(((vsa, vla, vrt, vfa), (vsb, vlt, vrb, vfb))):
        for copy in copies[5 + 2 * h : 7 + 2 * h]:
            copy.wait()

        @pl.loop(0, half // tile)
        def _(j):
            cols = pl.ds(pl.multiple_of(j * tile, tile), tile)
            block = jnp.concatenate([r[:, cols] for r in refs], axis=0)
            total = jnp.dot(turned[...], block, preferred_element_type=F32) * scale
            to = pl.ds(pl.multiple_of(h * half + j * tile, tile), tile)
            for k in range(out.shape[0]):
                out[k, :, to] = total[k * rows : (k + 1) * rows].astype(BF16)


def times_turned(left, right):
    return lax.dot_general(left, right, (((1,), (1,)), ((), ())), preferred_element_type=F32)


def far_kernel(scale, fa, fb, w, dep, out_a, out_b, vfa, vfb, vw, sems):
    part, width = vw.shape
    half, quarter = width // 2, part // 2
    copies = fetch(
        [
            (fa, vfa),
            (fb, vfb),
            (w.at[:, :half], vw.at[:, :half]),
            (w.at[:, half:], vw.at[:, half:]),
        ],
        sems,
    )
    copies[0].wait()
    copies[1].wait()
    x = jnp.concatenate([vfa[:, half:], vfb[:, half:]], axis=1)
    g = 0.0
    for h, (u, out) in enumerate(((vfa, out_a), (vfb, out_b))):
        copies[2 + h].wait()
        block = vw[:, h * half : (h + 1) * half]
        out[:, :half] = (jnp.dot(x, block, preferred_element_type=F32) * scale).astype(BF16)
        g = g + times_turned(u[:, :half], block)
    g = (g * scale).astype(BF16)
    out_a[:, half:] = g[:, :quarter]
    out_b[:, half:] = g[:, quarter:]


def near_kernel(
    scale, xo, lt, rt, w, sa, la, sb, rb, dep, p0, g0, tr, tl, pr, pl_, vx, vlt, vrt, vw, vsa, vla, vsb, vrb, sems
):
    part, width = vw.shape
    count, half = vsa.shape
    tile = half // 2
    copies = fetch(
        [
            (xo, vx),
            (lt, vlt),
            (rt, vrt),
            (w.at[:, :half], vw.at[:, :half]),
            (w.at[:, half:], vw.at[:, half:]),
            (sa.at[:, :half], vsa),
            (la.at[:, :half], vla),
            (sb.at[:, :half], vsb),
            (rb.at[:, :half], vrb),
        ],
        sems,
    )
    for copy in copies[:3]:
        copy.wait()
    x = jnp.concatenate([vx[...], vlt[:, half:], vrt[:, half:]], axis=0)
    for h in range(2):
        copies[3 + h].wait()
        for t in range(2):
            at = h * half + t * tile
            cols = slice(t * tile, (t + 1) * tile)
            p = jnp.dot(x, vw[:, at : at + tile], preferred_element_type=F32) * scale
            p0[:, at : at + tile] = p[:count]
            if h == 0:
                tl[:, cols] = p[count : 2 * count].astype(BF16)
                pr[:, cols] = p[2 * count :]
            else:
                tr[:, cols] = p[2 * count :].astype(BF16)
                pl_[:, cols] = p[count : 2 * count]
    for copy in copies[5:]:
        copy.wait()
    up_a = jnp.concatenate([vsa[...], vla[...], vrt[:, :half]], axis=0)
    up_b = jnp.concatenate([vsb[...], vlt[:, :half], vrb[...]], axis=0)
    for k in range(0, part, 256):
        g = times_turned(up_a, vw[k : k + 256, :half]) + times_turned(up_b, vw[k : k + 256, half:])
        g = (g * scale).astype(BF16)
        g0[:, k : k + 256] = g[:count]
        tl[:, half + k : half + k + 256] = g[count : 2 * count]
        tr[:, half + k : half + k + 256] = g[2 * count :]


def pass_kernel(pr, pl_, in_a, in_b, dr, dl):
    half = pr.shape[1]
    dr[:, :half] = (pr[...] + in_a[:, :half].astype(F32)).astype(BF16)
    dr[:, half:] = in_a[:, half:]
    dl[:, :half] = (pl_[...] + in_b[:, :half].astype(F32)).astype(BF16)
    dl[:, half:] = in_b[:, half:]


def result_kernel(n_x, me_ref, tok_ref, rstd_ref, p0, g0, lt, ld, rt, rd, out_p, out_x, back):
    me = me_ref[0]
    width, part = tok_ref.shape[1], g0.shape[1]
    rows = part // (width // part)
    half, quarter = width // 2, part // 2
    rstd = rstd_ref[:, :1]
    for h, (l, r) in enumerate(((ld, rt), (lt, rd))):
        cols = slice(h * half, (h + 1) * half)
        total = p0[:, cols] + l[:, :half].astype(F32) + r[:, :half].astype(F32)
        out_p[:, cols] = (total * rstd).astype(BF16)
    for d in range(n_x):
        slot = lax.rem(me + d, n_x) * rows
        for k in range(part // rows):
            at = k * rows
            if d == 0:
                block = g0[:, at : at + rows]
            elif d == 1:
                block = rt[:, half + at : half + at + rows]
            elif d == 3:
                block = lt[:, half + at : half + at + rows]
            elif at < quarter:
                block = ld[:, half + at : half + at + rows]
            else:
                block = rd[:, half + at - quarter : half + at - quarter + rows]
            back[:, pl.ds(pl.multiple_of(slot + k * n_x * rows, rows), rows)] = block.astype(F32)
    g = back[...]
    xhat = tok_ref[...].astype(F32) * rstd
    mean = jnp.mean(g * xhat, axis=1, keepdims=True)
    out_x[...] = (g - xhat * mean).astype(BF16)


def step_kernel(parts_ref, weight_ref, gain_ref, dep_1, dep_2, out_w_ref, out_g_ref):
    gain = gain_ref[...].astype(F32)
    grad = jnp.sum(parts_ref[...].astype(F32), axis=0)
    w = weight_ref[...].astype(F32)
    slope = jnp.sum(grad * w, axis=1, keepdims=True)
    out_w_ref[...] = (w - step_rate * (column_of(gain) * grad)).astype(BF16)
    out_g_ref[...] = (gain - gain_rate * row_of(slope)).astype(BF16)


def mean_kernel(w_ref, pw_ref, g_ref, pg_ref, out_w_ref, out_g_ref):
    out_w_ref[...] = (0.5 * (w_ref[...].astype(F32) + pw_ref[...].astype(F32))).astype(BF16)
    out_g_ref[...] = (0.5 * (g_ref[...].astype(F32) + pg_ref[...].astype(F32))).astype(BF16)


def on_device(tokens, weight, gain, upstream, step):
    n_x, n_y = lax.axis_size("x"), lax.axis_size("yh")
    rows, width_out = weight.shape
    count, width_in = tokens.shape
    scale = 1.0 / math.sqrt(width_in)
    half = width_out // 2
    part = n_y * rows
    me = lax.axis_index("x").astype(jnp.int32).reshape(1)
    gain_row = gain.reshape(1, rows)
    flops = 2 * n_x * count * part * width_out
    moved = 2 * (n_x * count * (part + width_out) + part * width_out)
    quarter = part // 2
    vmem = lambda *shape: pltpu.VMEM(shape, BF16)
    sems = lambda n: pltpu.SemaphoreType.DMA((n,))
    short, long = in_hbm((count, half + quarter)), in_hbm((count, half + part))

    (copies,) = call(
        weight_kernel,
        [(weight, BLOCK), (gain_row, BLOCK)],
        [in_hbm((n_y, rows, width_out))],
    )
    full_weight = exchange(copies, "yh").reshape(part, width_out)

    x_own, sa, sb, ta, tb, rstd = call(
        functools.partial(token_kernel, n_x),
        [(me, SCALAR), (tokens, BLOCK), (upstream, BLOCK), (copies, ANY)],
        [in_hbm((count, part)), short, short, long, long, in_hbm((count, 128), F32)],
    )
    la, rb = shifted(sa, "x", 1), shifted(sb, "x", -1)
    lt, rt = shifted(ta, "x", 1), shifted(tb, "x", -1)
    fa, fb = shifted(la, "x", 1), shifted(rb, "x", -1)

    (part_w,) = call(
        functools.partial(grad_kernel, scale),
        [(v, ANY) for v in (x_own, lt, rt, fa, fb, sa, la, sb, rb)],
        [in_hbm((n_y, rows, width_out))],
        [vmem(count, part)]
        + [vmem(count, half + part)] * 2
        + [vmem(count, half + quarter)] * 2
        + [vmem(count, half)] * 4
        + [vmem(part, n_x * count), sems(9)],
        flops,
        moved,
    )
    pieces_w = exchange(part_w, "yh")

    out_a, out_b = call(
        functools.partial(far_kernel, scale),
        [(v, ANY) for v in (fa, fb, full_weight, part_w)],
        [short, short],
        [vmem(count, half + quarter)] * 2 + [vmem(part, width_out), sems(4)],
        flops // 2,
        moved // 2,
    )
    in_a, in_b = shifted(out_a, "x", 1), shifted(out_b, "x", -1)
    p0, g0, tr, tl, pr, pl_ = call(
        functools.partial(near_kernel, scale),
        [(v, ANY) for v in (x_own, lt, rt, full_weight, sa, la, sb, rb, out_a)],
        [in_hbm((count, width_out), F32), in_hbm((count, part)), long, long]
        + [in_hbm((count, half), F32)] * 2,
        [vmem(count, part)]
        + [vmem(count, half + part)] * 2
        + [vmem(part, width_out)]
        + [vmem(count, half)] * 4
        + [sems(9)],
        2 * flops,
        2 * moved,
    )
    got_lt, got_rt = shifted(tr, "x", 1), shifted(tl, "x", -1)
    dr, dl = call(
        pass_kernel,
        [(pr, BLOCK), (pl_, BLOCK), (in_a, BLOCK), (in_b, BLOCK)],
        [short, short],
        moved=moved,
    )
    got_ld, got_rd = shifted(dr, "x", 1), shifted(dl, "x", -1)

    stepped_w, stepped_g = call(
        step_kernel,
        [(pieces_w, BLOCK), (weight, BLOCK), (gain_row, BLOCK), (got_ld, ANY), (got_rd, ANY)],
        [in_hbm((rows, width_out)), in_hbm((1, rows))],
        moved=moved,
    )

    def gossip(distance):
        def branch(params, rest):
            peers = jax.tree.map(lambda part: shifted(part, "rep", distance), params)
            results = call(
                functools.partial(result_kernel, n_x),
                [(rest[0], SCALAR)] + [(v, BLOCK) for v in rest[1:]],
                [in_hbm((count, width_out)), in_hbm((count, width_in))],
                [pltpu.VMEM((count, width_in), F32)],
                moved=moved,
            )
            return peers, results

        return branch

    (peer_w, peer_g), (projected, input_gradient) = lax.switch(
        step[0] % 4,
        [gossip(distance) for distance in (1, 2, 4, 8)],
        (stepped_w, stepped_g),
        (me, tokens, rstd, p0, g0, got_lt, got_ld, got_rt, got_rd),
    )
    new_weight, new_gain = call(
        mean_kernel,
        [(stepped_w, BLOCK), (peer_w, BLOCK), (stepped_g, BLOCK), (peer_g, BLOCK)],
        [in_hbm((rows, width_out)), in_hbm((1, rows))],
    )
    return (projected, input_gradient, new_weight, new_gain.reshape(rows))


def solution(mesh):
    n_rep, n_fsdp = mesh.devices.shape
    n_x = 4
    split = Mesh(mesh.devices.reshape(n_rep, n_fsdp // n_x, n_x), ("rep", "yh", "x"))
    every = ("rep", "yh", "x")
    placed = (P(every, None), P(every, None), P(every), P(every, None), P())
    return jax.shard_map(
        on_device,
        mesh=split,
        in_specs=placed,
        out_specs=(P(every, None), P(every, None), P(every, None), P(every)),
        check_vma=False,
    )
```

```python
import functools
import math

import jax
import jax.numpy as jnp
from jax import lax
from jax.experimental import pallas as pl
from jax.experimental.pallas import tpu as pltpu
from jax.sharding import Mesh
from jax.sharding import PartitionSpec as P

eps = 1e-05
step_rate = 0.75
gain_rate = 0.004
F32 = jnp.float32
BF16 = jnp.bfloat16
VMEM_LIMIT = 32 * 1024 * 1024
ANY = pl.BlockSpec(memory_space=pl.ANY)
DEP = pl.BlockSpec(memory_space=pl.ANY)
BLOCK, AUTO = "block", "auto"
HERE = pl.BlockSpec(memory_space=pltpu.VMEM)
SCALAR = pl.BlockSpec(memory_space=pltpu.SMEM)


def array(shape, dtype=BF16):
    return jax.ShapeDtypeStruct(shape, dtype)


def in_hbm(shape, dtype=BF16):
    return pltpu.HBM(shape, dtype)


def call(kernel, ins, outs, scratch=(), flops=0, moved=0, passed={}):
    values = [
        pltpu.with_memory_space_constraint(v, pltpu.HBM) if spec is ANY or spec is BLOCK else v
        for v, spec in ins
    ]
    return pl.pallas_call(
        kernel,
        grid=(1,),
        out_shape=list(outs),
        in_specs=[whole(v.shape) if spec in (BLOCK, AUTO) else spec for v, spec in ins],
        out_specs=[
            DEP if i in passed.values() else HERE if isinstance(shape, jax.ShapeDtypeStruct) else whole(shape.shape)
            for i, shape in enumerate(outs)
        ],
        input_output_aliases=passed,
        scratch_shapes=list(scratch),
        compiler_params=pltpu.CompilerParams(vmem_limit_bytes=VMEM_LIMIT),
        cost_estimate=pl.CostEstimate(flops=flops, bytes_accessed=moved, transcendentals=0),
    )(*values)


def whole(shape):
    return pl.BlockSpec(shape, lambda s: (0,) * len(shape))


def fetch(pairs, sems):
    copies = [pltpu.make_async_copy(src, dst, sems.at[i]) for i, (src, dst) in enumerate(pairs)]
    for copy in copies:
        copy.start()
    return copies


def shifted(value, axis, steps):
    count = lax.axis_size(axis)
    pairs = [(source, (source + steps) % count) for source in range(count)]
    return lax.ppermute(value, axis, pairs)


def exchange(blocks, axis):
    return lax.all_to_all(blocks, axis, split_axis=0, concat_axis=0, tiled=True)


def column_of(row):
    n = row.shape[1]
    down = lax.broadcasted_iota(jnp.int32, (n, n), 0)
    along = lax.broadcasted_iota(jnp.int32, (n, n), 1)
    return jnp.sum(jnp.where(down == along, row, 0.0), axis=1, keepdims=True)


def row_of(column):
    n = column.shape[0]
    down = lax.broadcasted_iota(jnp.int32, (n, n), 0)
    along = lax.broadcasted_iota(jnp.int32, (n, n), 1)
    return jnp.sum(jnp.where(down == along, column, 0.0), axis=0, keepdims=True)


def weight_kernel(gain_ref, weight_ref, out_ref):
    scaled = (weight_ref[...].astype(F32) * column_of(gain_ref[...].astype(F32))).astype(BF16)
    for i in range(out_ref.shape[0]):
        out_ref[i] = scaled


def token_kernel(
    n_x, me_ref, tok, up, dep, own_ref, sa_ref, sb_ref, ta_ref, tb_ref, rstd_ref, vt, vu, sems
):
    fetched = fetch([(tok, vt), (up, vu)], sems)
    me = me_ref[0]
    width, part = vt.shape[1], own_ref.shape[1]
    rows = part // (width // part)
    half, quarter = width // 2, part // 2
    fetched[0].wait()
    for d in range(n_x):
        slot = lax.rem(me + d, n_x) * rows
        for k in range(part // rows):
            block = vt[:, pl.ds(pl.multiple_of(slot + k * n_x * rows, rows), rows)]
            at = k * rows
            if d == 0:
                own_ref[:, at : at + rows] = block
            elif d == 1:
                ta_ref[:, half + at : half + at + rows] = block
            elif d == 3:
                tb_ref[:, half + at : half + at + rows] = block
            elif at < quarter:
                sa_ref[:, half + at : half + at + rows] = block
            else:
                sb_ref[:, half + at - quarter : half + at - quarter + rows] = block
    x = vt[...].astype(F32)
    rstd = lax.rsqrt(jnp.mean(x * x, axis=1, keepdims=True) + eps)
    rstd_ref[...] = jnp.broadcast_to(rstd, rstd_ref.shape)
    fetched[1].wait()
    up_a = (vu[:, :half].astype(F32) * rstd).astype(BF16)
    up_b = (vu[:, half:].astype(F32) * rstd).astype(BF16)
    sa_ref[:, :half] = up_a
    tb_ref[:, :half] = up_a
    sb_ref[:, :half] = up_b
    ta_ref[:, :half] = up_b


def grad_kernel(xo, lt, rt, sa, la, sb, rb, out, vx, vlt, vrt, vsa, vla, vsb, vrb, turned, sems):
    half = vsa.shape[1]
    tile = 256
    copies = fetch(
        [
            (xo, vx),
            (lt, vlt),
            (rt, vrt),
            (sa.at[:, :half], vsa),
            (la.at[:, :half], vla),
            (sb.at[:, :half], vsb),
            (rb.at[:, :half], vrb),
        ],
        sems,
    )
    for copy in copies[:3]:
        copy.wait()
    turned[...] = jnp.concatenate([vx[...], vlt[:, half:], vrt[:, half:]], axis=0).T
    for h, refs in enumerate(((vsa, vla, vrt), (vsb, vlt, vrb))):
        for copy in copies[3 + 2 * h : 5 + 2 * h]:
            copy.wait()

        @pl.loop(0, half // tile)
        def _(j):
            cols = pl.ds(pl.multiple_of(j * tile, tile), tile)
            block = jnp.concatenate([r[:, cols] for r in refs], axis=0)
            to = pl.ds(pl.multiple_of(h * half + j * tile, tile), tile)
            out[:, to] = jnp.dot(turned[...], block, preferred_element_type=F32)


def grad_far_kernel(scale, near, fa, fb, out, turned):
    half = near.shape[1] // 2
    rows = out.shape[1]
    tile = 256
    turned[...] = jnp.concatenate([fa[:, half:], fb[:, half:]], axis=1).T
    for h, ref in enumerate((fa, fb)):

        @pl.loop(0, half // tile)
        def _(j):
            cols = pl.ds(pl.multiple_of(j * tile, tile), tile)
            to = pl.ds(pl.multiple_of(h * half + j * tile, tile), tile)
            total = near[:, to] + jnp.dot(turned[...], ref[:, cols], preferred_element_type=F32)
            total = (total * scale).astype(BF16)
            for k in range(out.shape[0]):
                out[k, :, to] = total[k * rows : (k + 1) * rows]


def times_turned(left, right):
    return lax.dot_general(left, right, (((1,), (1,)), ((), ())), preferred_element_type=F32)


def far_kernel(scale, fa, fb, w, dep, out_a, out_b, vw, sems):
    part, width = w.shape
    half, quarter = width // 2, part // 2
    pieces = [(w.at[:, i * half : (i + 1) * half], vw.at[:, i * half : (i + 1) * half]) for i in range(2)]
    copies = fetch(pieces, sems)
    x = jnp.concatenate([fa[:, half:], fb[:, half:]], axis=1)
    g = 0.0
    for h, (u, out) in enumerate(((fa, out_a), (fb, out_b))):
        copies[h].wait()
        block = vw[:, h * half : (h + 1) * half]
        out[:, :half] = (jnp.dot(x, block, preferred_element_type=F32) * scale).astype(BF16)
        g = g + times_turned(u[:, :half], block)
    g = (g * scale).astype(BF16)
    out_a[:, half:] = g[:, :quarter]
    out_b[:, half:] = g[:, quarter:]


def near_kernel(
    scale, xo, lt, rt, sa, la, sb, rb, w, dep, p0, g0, tr, tl, pr, pl_, vx, vlt, vrt, vsa, vla, vsb, vrb, vw, sems
):
    part = w.shape[0]
    count, half = vsa.shape
    tile = half // 2
    copies = fetch(
        [
            (xo, vx),
            (lt, vlt),
            (rt, vrt),
            (sa.at[:, :half], vsa),
            (la.at[:, :half], vla),
            (sb.at[:, :half], vsb),
            (rb.at[:, :half], vrb),
            (w.at[:, :half], vw.at[:, :half]),
            (w.at[:, half:], vw.at[:, half:]),
        ],
        sems,
    )
    for copy in copies[:3]:
        copy.wait()
    x = jnp.concatenate([vx[...], vlt[:, half:], vrt[:, half:]], axis=0)
    for h in range(2):
        copies[7 + h].wait()
        for t in range(2):
            at = h * half + t * tile
            cols = slice(t * tile, (t + 1) * tile)
            p = jnp.dot(x, vw[:, at : at + tile], preferred_element_type=F32) * scale
            p0[:, at : at + tile] = p[:count]
            if h == 0:
                tl[:, cols] = p[count : 2 * count].astype(BF16)
                pr[:, cols] = p[2 * count :]
            else:
                tr[:, cols] = p[2 * count :].astype(BF16)
                pl_[:, cols] = p[count : 2 * count]
    for copy in copies[3:7]:
        copy.wait()
    up_a = jnp.concatenate([vsa[...], vla[...], vrt[:, :half]], axis=0)
    up_b = jnp.concatenate([vsb[...], vlt[:, :half], vrb[...]], axis=0)
    for k in range(0, part, 256):
        g = times_turned(up_a, vw[k : k + 256, :half]) + times_turned(up_b, vw[k : k + 256, half:])
        g = (g * scale).astype(BF16)
        g0[:, k : k + 256] = g[:count]
        tl[:, half + k : half + k + 256] = g[count : 2 * count]
        tr[:, half + k : half + k + 256] = g[2 * count :]


def pass_kernel(pr, pl_, in_a, in_b, dr, dl):
    half = pr.shape[1]
    dr[:, :half] = (pr[...] + in_a[:, :half].astype(F32)).astype(BF16)
    dr[:, half:] = in_a[:, half:]
    dl[:, :half] = (pl_[...] + in_b[:, :half].astype(F32)).astype(BF16)
    dl[:, half:] = in_b[:, half:]


def result_kernel(n_x, me_ref, tok_ref, rstd_ref, p0, g0, lt, ld, rt, rd, out_p, out_x, back):
    me = me_ref[0]
    width, part = tok_ref.shape[1], g0.shape[1]
    rows = part // (width // part)
    half, quarter = width // 2, part // 2
    rstd = rstd_ref[:, :1]
    for h, (l, r) in enumerate(((ld, rt), (lt, rd))):
        cols = slice(h * half, (h + 1) * half)
        total = p0[:, cols] + l[:, :half].astype(F32) + r[:, :half].astype(F32)
        out_p[:, cols] = (total * rstd).astype(BF16)
    for d in range(n_x):
        slot = lax.rem(me + d, n_x) * rows
        for k in range(part // rows):
            at = k * rows
            if d == 0:
                block = g0[:, at : at + rows]
            elif d == 1:
                block = rt[:, half + at : half + at + rows]
            elif d == 3:
                block = lt[:, half + at : half + at + rows]
            elif at < quarter:
                block = ld[:, half + at : half + at + rows]
            else:
                block = rd[:, half + at - quarter : half + at - quarter + rows]
            back[:, pl.ds(pl.multiple_of(slot + k * n_x * rows, rows), rows)] = block.astype(F32)
    g = back[...]
    xhat = tok_ref[...].astype(F32) * rstd
    mean = jnp.mean(g * xhat, axis=1, keepdims=True)
    out_x[...] = (g - xhat * mean).astype(BF16)


def step_kernel(parts_ref, weight_ref, gain_ref, dep_1, dep_2, out_ref):
    width = weight_ref.shape[1]
    column = column_of(gain_ref[...].astype(F32))
    grad = jnp.sum(parts_ref[...].astype(F32), axis=0)
    w = weight_ref[...].astype(F32)
    slope = jnp.sum(grad * w, axis=1, keepdims=True)
    out_ref[:, :width] = (w - step_rate * (column * grad)).astype(BF16)
    stepped = (column - gain_rate * slope).astype(BF16)
    out_ref[:, width:] = jnp.broadcast_to(stepped, (stepped.shape[0], out_ref.shape[1] - width))


def mean_kernel(mine, peer, out_w_ref, out_g_ref):
    width = out_w_ref.shape[1]
    out_w_ref[...] = (0.5 * (mine[:, :width].astype(F32) + peer[:, :width].astype(F32))).astype(BF16)
    column = 0.5 * (mine[:, width : width + 1].astype(F32) + peer[:, width : width + 1].astype(F32))
    out_g_ref[...] = row_of(column).astype(BF16)


def on_device(tokens, weight, gain, upstream, step):
    n_x, n_y = lax.axis_size("x"), lax.axis_size("yh")
    rows, width_out = weight.shape
    count, width_in = tokens.shape
    scale = 1.0 / math.sqrt(width_in)
    half = width_out // 2
    part = n_y * rows
    me = jnp.stack([lax.axis_index("x"), lax.axis_index("yh")]).astype(jnp.int32)
    gain_row = gain.reshape(1, rows)
    flops = 2 * n_x * count * part * width_out
    moved = 2 * (n_x * count * (part + width_out) + part * width_out)
    quarter = part // 2
    vmem = lambda *shape: pltpu.VMEM(shape, BF16)
    sems = lambda n: pltpu.SemaphoreType.DMA((n,))
    short, long = (count, half + quarter), (count, half + part)

    (copies,) = call(
        weight_kernel, [(gain_row, BLOCK), (weight, BLOCK)], [in_hbm((n_y, rows, width_out))]
    )
    full_weight = exchange(copies, "yh").reshape(part, width_out)

    x_own, sa, sb, ta, tb, rstd = call(
        functools.partial(token_kernel, n_x),
        [(me, SCALAR), (tokens, ANY), (upstream, ANY), (copies, DEP)],
        [
            in_hbm((count, part)),
            in_hbm(short),
            in_hbm(short),
            array(long),
            array(long),
            in_hbm((count, 128), F32),
        ],
        [vmem(count, width_in), vmem(count, width_out), sems(2)],
    )
    la, rb = shifted(sa, "x", 1), shifted(sb, "x", -1)
    lt, rt = shifted(ta, "x", 1), shifted(tb, "x", -1)
    fa, fb = shifted(la, "x", 1), shifted(rb, "x", -1)

    near = [(v, ANY) for v in (x_own, lt, rt, sa, la, sb, rb)]
    near_scratch = [vmem(count, part)] + [vmem(*long)] * 2 + [vmem(count, half)] * 4
    (near_w,) = call(
        grad_kernel,
        near,
        [array((part, width_out), F32)],
        near_scratch + [vmem(part, 3 * count), sems(7)],
        flops * 3 // 4,
        moved,
    )
    (part_w,) = call(
        functools.partial(grad_far_kernel, scale),
        [(near_w, HERE), (fa, HERE), (fb, HERE)],
        [array((n_y, rows, width_out))],
        [vmem(part, count)],
        flops // 4,
        moved,
    )

    pieces_w = exchange(part_w, "yh")
    out_a, out_b = call(
        functools.partial(far_kernel, scale),
        [(fa, HERE), (fb, HERE), (full_weight, DEP), (part_w, DEP)],
        [array(short), array(short)],
        [vmem(part, width_out), sems(2)],
        flops // 2,
        moved // 2,
    )
    in_a, in_b = shifted(out_a, "x", 1), shifted(out_b, "x", -1)
    p0, g0, tr, tl, pr, pl_ = call(
        functools.partial(near_kernel, scale),
        near + [(full_weight, DEP), (out_a, DEP)],
        [in_hbm((count, width_out), F32), in_hbm((count, part)), array(long), array(long)]
        + [array((count, half), F32)] * 2,
        near_scratch + [vmem(part, width_out), sems(9)],
        2 * flops,
        2 * moved,
    )
    got_lt, got_rt = shifted(tr, "x", 1), shifted(tl, "x", -1)
    dr, dl = call(
        pass_kernel,
        [(pr, HERE), (pl_, HERE), (in_a, HERE), (in_b, HERE)],
        [array(short), array(short)],
        moved=moved,
    )
    got_ld, got_rd = shifted(dr, "x", 1), shifted(dl, "x", -1)

    (stepped,) = call(
        step_kernel,
        [(v, HERE) for v in (pieces_w, weight, gain_row)] + [(got_ld, DEP), (got_rd, DEP)],
        [array((rows, width_out + 128))],
        moved=moved,
    )

    def gossip(distance):
        def branch(stepped, rest):
            peer = shifted(stepped, "rep", distance)
            results = call(
                functools.partial(result_kernel, n_x),
                [(rest[0], SCALAR)] + [(v, BLOCK) for v in rest[1:]],
                [in_hbm((count, width_out)), in_hbm((count, width_in))],
                [pltpu.VMEM((count, width_in), F32)],
                moved=moved,
            )
            means = call(
                mean_kernel,
                [(stepped, HERE), (peer, HERE)],
                [in_hbm((rows, width_out)), in_hbm((1, rows))],
            )
            return *results, *means

        return branch

    projected, input_gradient, new_weight, new_gain = lax.switch(
        step[0] % 4,
        [gossip(distance) for distance in (1, 2, 4, 8)],
        stepped,
        (me, tokens, rstd, p0, g0, got_lt, got_ld, got_rt, got_rd),
    )
    return projected, input_gradient, new_weight, new_gain.reshape(rows)


def solution(mesh):
    n_rep, n_fsdp = mesh.devices.shape
    n_x = 4
    split = Mesh(mesh.devices.reshape(n_rep, n_fsdp // n_x, n_x), ("rep", "yh", "x"))
    every = ("rep", "yh", "x")
    placed = (P(every, None), P(every, None), P(every), P(every, None), P())
    return jax.shard_map(
        on_device,
        mesh=split,
        in_specs=placed,
        out_specs=(P(every, None), P(every, None), P(every, None), P(every)),
        check_vma=False,
    )
```

```python
import functools
import math

import jax
import jax.numpy as jnp
from jax import lax
from jax.experimental import pallas as pl
from jax.experimental.pallas import tpu as pltpu
from jax.sharding import Mesh
from jax.sharding import PartitionSpec as P

eps = 1e-05
step_rate = 0.75
gain_rate = 0.004
F32 = jnp.float32
BF16 = jnp.bfloat16
VMEM_LIMIT = 32 * 1024 * 1024
ANY = pl.BlockSpec(memory_space=pl.ANY)
DEP = pl.BlockSpec(memory_space=pl.ANY)
BLOCK, AUTO = "block", "auto"
HERE = pl.BlockSpec(memory_space=pltpu.VMEM)
SCALAR = pl.BlockSpec(memory_space=pltpu.SMEM)


def array(shape, dtype=BF16):
    return jax.ShapeDtypeStruct(shape, dtype)


def in_hbm(shape, dtype=BF16):
    return pltpu.HBM(shape, dtype)


def call(kernel, ins, outs, scratch=(), flops=0, moved=0, passed={}):
    values = [
        pltpu.with_memory_space_constraint(v, pltpu.HBM) if spec is ANY or spec is BLOCK else v
        for v, spec in ins
    ]
    return pl.pallas_call(
        kernel,
        grid=(1,),
        out_shape=list(outs),
        in_specs=[whole(v.shape) if spec in (BLOCK, AUTO) else spec for v, spec in ins],
        out_specs=[
            DEP if i in passed.values() else HERE if isinstance(shape, jax.ShapeDtypeStruct) else whole(shape.shape)
            for i, shape in enumerate(outs)
        ],
        input_output_aliases=passed,
        scratch_shapes=list(scratch),
        compiler_params=pltpu.CompilerParams(vmem_limit_bytes=VMEM_LIMIT),
        cost_estimate=pl.CostEstimate(flops=flops, bytes_accessed=moved, transcendentals=0),
    )(*values)


def whole(shape):
    return pl.BlockSpec(shape, lambda s: (0,) * len(shape))


def fetch(pairs, sems):
    copies = [pltpu.make_async_copy(src, dst, sems.at[i]) for i, (src, dst) in enumerate(pairs)]
    for copy in copies:
        copy.start()
    return copies


def shifted(value, axis, steps):
    count = lax.axis_size(axis)
    pairs = [(source, (source + steps) % count) for source in range(count)]
    return lax.ppermute(value, axis, pairs)


def exchange(blocks, axis):
    return lax.all_to_all(blocks, axis, split_axis=0, concat_axis=0, tiled=True)


def column_of(row):
    n = row.shape[1]
    down = lax.broadcasted_iota(jnp.int32, (n, n), 0)
    along = lax.broadcasted_iota(jnp.int32, (n, n), 1)
    return jnp.sum(jnp.where(down == along, row, 0.0), axis=1, keepdims=True)


def row_of(column):
    n = column.shape[0]
    down = lax.broadcasted_iota(jnp.int32, (n, n), 0)
    along = lax.broadcasted_iota(jnp.int32, (n, n), 1)
    return jnp.sum(jnp.where(down == along, column, 0.0), axis=0, keepdims=True)


def weight_kernel(gain_ref, weight_ref, out_ref):
    scaled = (weight_ref[...].astype(F32) * column_of(gain_ref[...].astype(F32))).astype(BF16)
    for i in range(out_ref.shape[0]):
        out_ref[i] = scaled


def token_kernel(
    n_x, me_ref, vt, vu, dep, own_ref, sa_ref, sb_ref, ta_ref, tb_ref, rstd_ref
):
    me = me_ref[0]
    width, part = vt.shape[1], own_ref.shape[1]
    rows = part // (width // part)
    half, quarter = width // 2, part // 2
    for d in range(n_x):
        slot = lax.rem(me + d, n_x) * rows
        for k in range(part // rows):
            block = vt[:, pl.ds(pl.multiple_of(slot + k * n_x * rows, rows), rows)]
            at = k * rows
            if d == 0:
                own_ref[:, at : at + rows] = block
            elif d == 1:
                ta_ref[:, half + at : half + at + rows] = block
            elif d == 3:
                tb_ref[:, half + at : half + at + rows] = block
            elif at < quarter:
                sa_ref[:, half + at : half + at + rows] = block
            else:
                sb_ref[:, half + at - quarter : half + at - quarter + rows] = block
    x = vt[...].astype(F32)
    rstd = lax.rsqrt(jnp.mean(x * x, axis=1, keepdims=True) + eps)
    rstd_ref[...] = jnp.broadcast_to(rstd, rstd_ref.shape)
    up_a = (vu[:, :half].astype(F32) * rstd).astype(BF16)
    up_b = (vu[:, half:].astype(F32) * rstd).astype(BF16)
    sa_ref[:, :half] = up_a
    tb_ref[:, :half] = up_a
    sb_ref[:, :half] = up_b
    ta_ref[:, :half] = up_b


def grad_kernel(xo, lt, rt, sa, la, sb, rb, out, vx, vlt, vrt, vsa, vla, vsb, vrb, turned, sems):
    half = vsa.shape[1]
    tile = 256
    copies = fetch(
        [
            (xo, vx),
            (lt, vlt),
            (rt, vrt),
            (sa.at[:, :half], vsa),
            (la.at[:, :half], vla),
            (sb.at[:, :half], vsb),
            (rb.at[:, :half], vrb),
        ],
        sems,
    )
    for copy in copies[:3]:
        copy.wait()
    turned[...] = jnp.concatenate([vx[...], vlt[:, half:], vrt[:, half:]], axis=0).T
    for h, refs in enumerate(((vsa, vla, vrt), (vsb, vlt, vrb))):
        for copy in copies[3 + 2 * h : 5 + 2 * h]:
            copy.wait()

        @pl.loop(0, half // tile)
        def _(j):
            cols = pl.ds(pl.multiple_of(j * tile, tile), tile)
            block = jnp.concatenate([r[:, cols] for r in refs], axis=0)
            to = pl.ds(pl.multiple_of(h * half + j * tile, tile), tile)
            out[:, to] = jnp.dot(turned[...], block, preferred_element_type=F32)


def grad_far_kernel(scale, near, fa, fb, out, turned):
    half = near.shape[1] // 2
    rows = out.shape[1]
    tile = 256
    turned[...] = jnp.concatenate([fa[:, half:], fb[:, half:]], axis=1).T
    for h, ref in enumerate((fa, fb)):

        @pl.loop(0, half // tile)
        def _(j):
            cols = pl.ds(pl.multiple_of(j * tile, tile), tile)
            to = pl.ds(pl.multiple_of(h * half + j * tile, tile), tile)
            total = near[:, to] + jnp.dot(turned[...], ref[:, cols], preferred_element_type=F32)
            total = (total * scale).astype(BF16)
            for k in range(out.shape[0]):
                out[k, :, to] = total[k * rows : (k + 1) * rows]


def times_turned(left, right):
    return lax.dot_general(left, right, (((1,), (1,)), ((), ())), preferred_element_type=F32)


def far_kernel(scale, fa, fb, w, dep, out_a, out_b, vw, sems):
    part, width = w.shape
    half, quarter = width // 2, part // 2
    pieces = [(w.at[:, i * half : (i + 1) * half], vw.at[:, i * half : (i + 1) * half]) for i in range(2)]
    copies = fetch(pieces, sems)
    x = jnp.concatenate([fa[:, half:], fb[:, half:]], axis=1)
    g = 0.0
    for h, (u, out) in enumerate(((fa, out_a), (fb, out_b))):
        copies[h].wait()
        block = vw[:, h * half : (h + 1) * half]
        out[:, :half] = (jnp.dot(x, block, preferred_element_type=F32) * scale).astype(BF16)
        g = g + times_turned(u[:, :half], block)
    g = (g * scale).astype(BF16)
    out_a[:, half:] = g[:, :quarter]
    out_b[:, half:] = g[:, quarter:]


def near_kernel(
    scale, xo, lt, rt, sa, la, sb, rb, w, dep, p0, g0, tr, tl, pr, pl_, vx, vlt, vrt, vsa, vla, vsb, vrb, vw, sems
):
    part = w.shape[0]
    count, half = vsa.shape
    tile = half // 2
    copies = fetch(
        [
            (xo, vx),
            (lt, vlt),
            (rt, vrt),
            (sa.at[:, :half], vsa),
            (la.at[:, :half], vla),
            (sb.at[:, :half], vsb),
            (rb.at[:, :half], vrb),
            (w.at[:, :half], vw.at[:, :half]),
            (w.at[:, half:], vw.at[:, half:]),
        ],
        sems,
    )
    for copy in copies[:3]:
        copy.wait()
    x = jnp.concatenate([vx[...], vlt[:, half:], vrt[:, half:]], axis=0)
    for h in range(2):
        copies[7 + h].wait()
        for t in range(2):
            at = h * half + t * tile
            cols = slice(t * tile, (t + 1) * tile)
            p = jnp.dot(x, vw[:, at : at + tile], preferred_element_type=F32) * scale
            p0[:, at : at + tile] = p[:count]
            if h == 0:
                tl[:, cols] = p[count : 2 * count].astype(BF16)
                pr[:, cols] = p[2 * count :]
            else:
                tr[:, cols] = p[2 * count :].astype(BF16)
                pl_[:, cols] = p[count : 2 * count]
    for copy in copies[3:7]:
        copy.wait()
    up_a = jnp.concatenate([vsa[...], vla[...], vrt[:, :half]], axis=0)
    up_b = jnp.concatenate([vsb[...], vlt[:, :half], vrb[...]], axis=0)
    for k in range(0, part, 256):
        g = times_turned(up_a, vw[k : k + 256, :half]) + times_turned(up_b, vw[k : k + 256, half:])
        g = (g * scale).astype(BF16)
        g0[:, k : k + 256] = g[:count]
        tl[:, half + k : half + k + 256] = g[count : 2 * count]
        tr[:, half + k : half + k + 256] = g[2 * count :]


def pass_kernel(pr, pl_, in_a, in_b, dr, dl):
    half = pr.shape[1]
    dr[:, :half] = (pr[...] + in_a[:, :half].astype(F32)).astype(BF16)
    dr[:, half:] = in_a[:, half:]
    dl[:, :half] = (pl_[...] + in_b[:, :half].astype(F32)).astype(BF16)
    dl[:, half:] = in_b[:, half:]


def result_kernel(n_x, me_ref, tok_ref, rstd_ref, p0, g0, lt, ld, rt, rd, out_p, out_x, back):
    me = me_ref[0]
    width, part = tok_ref.shape[1], g0.shape[1]
    rows = part // (width // part)
    half, quarter = width // 2, part // 2
    rstd = rstd_ref[:, :1]
    for h, (l, r) in enumerate(((ld, rt), (lt, rd))):
        cols = slice(h * half, (h + 1) * half)
        total = p0[:, cols] + l[:, :half].astype(F32) + r[:, :half].astype(F32)
        out_p[:, cols] = (total * rstd).astype(BF16)
    for d in range(n_x):
        slot = lax.rem(me + d, n_x) * rows
        for k in range(part // rows):
            at = k * rows
            if d == 0:
                block = g0[:, at : at + rows]
            elif d == 1:
                block = rt[:, half + at : half + at + rows]
            elif d == 3:
                block = lt[:, half + at : half + at + rows]
            elif at < quarter:
                block = ld[:, half + at : half + at + rows]
            else:
                block = rd[:, half + at - quarter : half + at - quarter + rows]
            back[:, pl.ds(pl.multiple_of(slot + k * n_x * rows, rows), rows)] = block.astype(F32)
    g = back[...]
    xhat = tok_ref[...].astype(F32) * rstd
    mean = jnp.mean(g * xhat, axis=1, keepdims=True)
    out_x[...] = (g - xhat * mean).astype(BF16)


def step_kernel(parts_ref, weight_ref, gain_ref, dep_1, dep_2, out_w_ref, out_g_ref):
    gain = gain_ref[...].astype(F32)
    grad = jnp.sum(parts_ref[...].astype(F32), axis=0)
    w = weight_ref[...].astype(F32)
    slope = jnp.sum(grad * w, axis=1, keepdims=True)
    out_w_ref[...] = (w - step_rate * (column_of(gain) * grad)).astype(BF16)
    out_g_ref[...] = (gain - gain_rate * row_of(slope)).astype(BF16)


def mean_kernel(w_ref, pw_ref, g_ref, pg_ref, out_w_ref, out_g_ref):
    out_w_ref[...] = (0.5 * (w_ref[...].astype(F32) + pw_ref[...].astype(F32))).astype(BF16)
    out_g_ref[...] = (0.5 * (g_ref[...].astype(F32) + pg_ref[...].astype(F32))).astype(BF16)


def on_device(tokens, weight, gain, upstream, step):
    n_x, n_y = lax.axis_size("x"), lax.axis_size("yh")
    rows, width_out = weight.shape
    count, width_in = tokens.shape
    scale = 1.0 / math.sqrt(width_in)
    half = width_out // 2
    part = n_y * rows
    me = jnp.stack([lax.axis_index("x"), lax.axis_index("yh")]).astype(jnp.int32)
    gain_row = gain.reshape(1, rows)
    flops = 2 * n_x * count * part * width_out
    moved = 2 * (n_x * count * (part + width_out) + part * width_out)
    quarter = part // 2
    vmem = lambda *shape: pltpu.VMEM(shape, BF16)
    sems = lambda n: pltpu.SemaphoreType.DMA((n,))
    short, long = (count, half + quarter), (count, half + part)

    (copies,) = call(
        weight_kernel, [(gain_row, BLOCK), (weight, BLOCK)], [in_hbm((n_y, rows, width_out))]
    )
    full_weight = exchange(copies, "yh").reshape(part, width_out)

    x_own, sa, sb, ta, tb, rstd = call(
        functools.partial(token_kernel, n_x),
        [(me, SCALAR), (tokens, HERE), (upstream, HERE), (copies, DEP)],
        [
            in_hbm((count, part)),
            in_hbm(short),
            in_hbm(short),
            array(long),
            array(long),
            in_hbm((count, 128), F32),
        ],
    )
    la, rb = shifted(sa, "x", 1), shifted(sb, "x", -1)
    lt, rt = shifted(ta, "x", 1), shifted(tb, "x", -1)
    fa, fb = shifted(la, "x", 1), shifted(rb, "x", -1)

    near = [(v, ANY) for v in (x_own, lt, rt, sa, la, sb, rb)]
    near_scratch = [vmem(count, part)] + [vmem(*long)] * 2 + [vmem(count, half)] * 4
    (near_w,) = call(
        grad_kernel,
        near,
        [array((part, width_out), F32)],
        near_scratch + [vmem(part, 3 * count), sems(7)],
        flops * 3 // 4,
        moved,
    )
    (part_w,) = call(
        functools.partial(grad_far_kernel, scale),
        [(near_w, HERE), (fa, HERE), (fb, HERE)],
        [array((n_y, rows, width_out))],
        [vmem(part, count)],
        flops // 4,
        moved,
    )

    pieces_w = exchange(part_w, "yh")
    out_a, out_b = call(
        functools.partial(far_kernel, scale),
        [(fa, HERE), (fb, HERE), (full_weight, DEP), (part_w, DEP)],
        [array(short), array(short)],
        [vmem(part, width_out), sems(2)],
        flops // 2,
        moved // 2,
    )
    in_a, in_b = shifted(out_a, "x", 1), shifted(out_b, "x", -1)
    p0, g0, tr, tl, pr, pl_ = call(
        functools.partial(near_kernel, scale),
        near + [(full_weight, DEP), (out_a, DEP)],
        [in_hbm((count, width_out), F32), in_hbm((count, part)), array(long), array(long)]
        + [array((count, half), F32)] * 2,
        near_scratch + [vmem(part, width_out), sems(9)],
        2 * flops,
        2 * moved,
    )
    got_lt, got_rt = shifted(tr, "x", 1), shifted(tl, "x", -1)
    dr, dl = call(
        pass_kernel,
        [(pr, HERE), (pl_, HERE), (in_a, HERE), (in_b, HERE)],
        [array(short), array(short)],
        moved=moved,
    )
    got_ld, got_rd = shifted(dr, "x", 1), shifted(dl, "x", -1)

    stepped = call(
        step_kernel,
        [(v, HERE) for v in (pieces_w, weight, gain_row)] + [(got_ld, DEP), (got_rd, DEP)],
        [array((rows, width_out)), array((1, rows))],
        moved=moved,
    )

    def gossip(distance):
        def branch(stepped, rest):
            peer = [shifted(v, "rep", distance) for v in stepped]
            results = call(
                functools.partial(result_kernel, n_x),
                [(rest[0], SCALAR)] + [(v, BLOCK) for v in rest[1:]],
                [in_hbm((count, width_out)), in_hbm((count, width_in))],
                [pltpu.VMEM((count, width_in), F32)],
                moved=moved,
            )
            means = call(
                mean_kernel,
                [(v, HERE) for v in (stepped[0], peer[0], stepped[1], peer[1])],
                [in_hbm((rows, width_out)), in_hbm((1, rows))],
            )
            return *results, *means

        return branch

    projected, input_gradient, new_weight, new_gain = lax.switch(
        step[0] % 4,
        [gossip(distance) for distance in (1, 2, 4, 8)],
        stepped,
        (me, tokens, rstd, p0, g0, got_lt, got_ld, got_rt, got_rd),
    )
    return projected, input_gradient, new_weight, new_gain.reshape(rows)


def solution(mesh):
    n_rep, n_fsdp = mesh.devices.shape
    n_x = 4
    split = Mesh(mesh.devices.reshape(n_rep, n_fsdp // n_x, n_x), ("rep", "yh", "x"))
    every = ("rep", "yh", "x")
    placed = (P(every, None), P(every, None), P(every), P(every, None), P())
    return jax.shard_map(
        on_device,
        mesh=split,
        in_specs=placed,
        out_specs=(P(every, None), P(every, None), P(every, None), P(every)),
        check_vma=False,
    )
```

```python
import functools
import math

import jax
import jax.numpy as jnp
from jax import lax
from jax.experimental import pallas as pl
from jax.experimental.pallas import tpu as pltpu
from jax.sharding import Mesh
from jax.sharding import PartitionSpec as P

eps = 1e-05
step_rate = 0.75
gain_rate = 0.004
F32 = jnp.float32
BF16 = jnp.bfloat16
VMEM_LIMIT = 32 * 1024 * 1024
ANY = pl.BlockSpec(memory_space=pl.ANY)
DEP = pl.BlockSpec(memory_space=pl.ANY)
BLOCK, AUTO = "block", "auto"
HERE = pl.BlockSpec(memory_space=pltpu.VMEM)
SCALAR = pl.BlockSpec(memory_space=pltpu.SMEM)


def array(shape, dtype=BF16):
    return jax.ShapeDtypeStruct(shape, dtype)


def in_hbm(shape, dtype=BF16):
    return pltpu.HBM(shape, dtype)


def call(kernel, ins, outs, scratch=(), flops=0, moved=0):
    values = [
        pltpu.with_memory_space_constraint(v, pltpu.HBM) if spec is ANY or spec is BLOCK else v
        for v, spec in ins
    ]

    def out_spec(shape):
        if isinstance(shape, tuple):
            return ANY
        return HERE if isinstance(shape, jax.ShapeDtypeStruct) else whole(shape.shape)

    return pl.pallas_call(
        kernel,
        grid=(1,),
        out_shape=[shape[0] if isinstance(shape, tuple) else shape for shape in outs],
        in_specs=[whole(v.shape) if spec in (BLOCK, AUTO) else spec for v, spec in ins],
        out_specs=[out_spec(shape) for shape in outs],
        scratch_shapes=list(scratch),
        compiler_params=pltpu.CompilerParams(vmem_limit_bytes=VMEM_LIMIT),
        cost_estimate=pl.CostEstimate(flops=flops, bytes_accessed=moved, transcendentals=0),
    )(*values)


def whole(shape):
    return pl.BlockSpec(shape, lambda s: (0,) * len(shape))


def fetch(pairs, sems):
    copies = [pltpu.make_async_copy(src, dst, sems.at[i]) for i, (src, dst) in enumerate(pairs)]
    for copy in copies:
        copy.start()
    return copies


def shifted(value, axis, steps):
    count = lax.axis_size(axis)
    pairs = [(source, (source + steps) % count) for source in range(count)]
    return lax.ppermute(value, axis, pairs)


def exchange(blocks, axis):
    return lax.all_to_all(blocks, axis, split_axis=0, concat_axis=0, tiled=True)


def column_of(row):
    n = row.shape[1]
    down = lax.broadcasted_iota(jnp.int32, (n, n), 0)
    along = lax.broadcasted_iota(jnp.int32, (n, n), 1)
    return jnp.sum(jnp.where(down == along, row, 0.0), axis=1, keepdims=True)


def row_of(column):
    n = column.shape[0]
    down = lax.broadcasted_iota(jnp.int32, (n, n), 0)
    along = lax.broadcasted_iota(jnp.int32, (n, n), 1)
    return jnp.sum(jnp.where(down == along, column, 0.0), axis=0, keepdims=True)


def weight_kernel(gain_ref, weight_ref, out_ref):
    scaled = (weight_ref[...].astype(F32) * column_of(gain_ref[...].astype(F32))).astype(BF16)
    for i in range(out_ref.shape[0]):
        out_ref[i] = scaled


def token_kernel(
    n_x, me_ref, vt, vu, dep, own_ref, sa_ref, sb_ref, ta_ref, tb_ref, rstd_ref
):
    me = me_ref[0]
    width, part = vt.shape[1], own_ref.shape[1]
    rows = part // (width // part)
    half, quarter = width // 2, part // 2
    for d in range(n_x):
        slot = lax.rem(me + d, n_x) * rows
        for k in range(part // rows):
            block = vt[:, pl.ds(pl.multiple_of(slot + k * n_x * rows, rows), rows)]
            at = k * rows
            if d == 0:
                own_ref[:, at : at + rows] = block
            elif d == 1:
                ta_ref[:, half + at : half + at + rows] = block
            elif d == 3:
                tb_ref[:, half + at : half + at + rows] = block
            elif at < quarter:
                sa_ref[:, half + at : half + at + rows] = block
            else:
                sb_ref[:, half + at - quarter : half + at - quarter + rows] = block
    x = vt[...].astype(F32)
    rstd = lax.rsqrt(jnp.mean(x * x, axis=1, keepdims=True) + eps)
    rstd_ref[...] = jnp.broadcast_to(rstd, rstd_ref.shape)
    up_a = (vu[:, :half].astype(F32) * rstd).astype(BF16)
    up_b = (vu[:, half:].astype(F32) * rstd).astype(BF16)
    sa_ref[:, :half] = up_a
    tb_ref[:, :half] = up_a
    sb_ref[:, :half] = up_b
    ta_ref[:, :half] = up_b


def grad_kernel(xo, lt, rt, sa, la, sb, rb, out, vx, vlt, vrt, vsa, vla, vsb, vrb, turned, sems):
    half = vsa.shape[1]
    tile = 256
    copies = fetch(
        [
            (xo, vx),
            (lt, vlt),
            (rt, vrt),
            (sa.at[:, :half], vsa),
            (la.at[:, :half], vla),
            (sb.at[:, :half], vsb),
            (rb.at[:, :half], vrb),
        ],
        sems,
    )
    for copy in copies[:3]:
        copy.wait()
    turned[...] = jnp.concatenate([vx[...], vlt[:, half:], vrt[:, half:]], axis=0).T
    for h, refs in enumerate(((vsa, vla, vrt), (vsb, vlt, vrb))):
        for copy in copies[3 + 2 * h : 5 + 2 * h]:
            copy.wait()

        @pl.loop(0, half // tile)
        def _(j):
            cols = pl.ds(pl.multiple_of(j * tile, tile), tile)
            block = jnp.concatenate([r[:, cols] for r in refs], axis=0)
            to = pl.ds(pl.multiple_of(h * half + j * tile, tile), tile)
            out[:, to] = jnp.dot(turned[...], block, preferred_element_type=F32)


def grad_far_kernel(scale, near, fa, fb, out, turned, total, sems):
    half = near.shape[1] // 2
    rows = out.shape[1]
    tile = 256
    turned[...] = jnp.concatenate([fa[:, half:], fb[:, half:]], axis=1).T
    copies = []
    for h, ref in enumerate((fa, fb)):

        @pl.loop(0, half // tile)
        def _(j):
            cols = pl.ds(pl.multiple_of(j * tile, tile), tile)
            to = pl.ds(pl.multiple_of(h * half + j * tile, tile), tile)
            part = near[:, to] + jnp.dot(turned[...], ref[:, cols], preferred_element_type=F32)
            part = (part * scale).astype(BF16)
            for k in range(out.shape[0]):
                total[h, k, :, cols] = part[k * rows : (k + 1) * rows]

        copy = pltpu.make_async_copy(
            total.at[h], out.at[:, :, h * half : (h + 1) * half], sems.at[h]
        )
        copy.start()
        copies.append(copy)
    for copy in copies:
        copy.wait()


def times_turned(left, right):
    return lax.dot_general(left, right, (((1,), (1,)), ((), ())), preferred_element_type=F32)


def far_kernel(scale, fa, fb, w, out_a, out_b, vw, sems):
    part, width = w.shape
    half, quarter = width // 2, part // 2
    pieces = [(w.at[:, i * half : (i + 1) * half], vw.at[:, i * half : (i + 1) * half]) for i in range(2)]
    copies = fetch(pieces, sems)
    x = jnp.concatenate([fa[:, half:], fb[:, half:]], axis=1)
    g = 0.0
    for h, (u, out) in enumerate(((fa, out_a), (fb, out_b))):
        copies[h].wait()
        block = vw[:, h * half : (h + 1) * half]
        out[:, :half] = (jnp.dot(x, block, preferred_element_type=F32) * scale).astype(BF16)
        g = g + times_turned(u[:, :half], block)
    g = (g * scale).astype(BF16)
    out_a[:, half:] = g[:, :quarter]
    out_b[:, half:] = g[:, quarter:]


def near_kernel(
    scale, xo, lt, rt, sa, la, sb, rb, w, dep, p0, g0, tr, tl, pr, pl_, vx, vlt, vrt, vsa, vla, vsb, vrb, vw, sems
):
    part = w.shape[0]
    count, half = vsa.shape
    tile = half // 2
    copies = fetch(
        [
            (xo, vx),
            (lt, vlt),
            (rt, vrt),
            (sa.at[:, :half], vsa),
            (la.at[:, :half], vla),
            (sb.at[:, :half], vsb),
            (rb.at[:, :half], vrb),
            (w.at[:, :half], vw.at[:, :half]),
            (w.at[:, half:], vw.at[:, half:]),
        ],
        sems,
    )
    for copy in copies[:3]:
        copy.wait()
    x = jnp.concatenate([vx[...], vlt[:, half:], vrt[:, half:]], axis=0)
    for h in range(2):
        copies[7 + h].wait()
        for t in range(2):
            at = h * half + t * tile
            cols = slice(t * tile, (t + 1) * tile)
            p = jnp.dot(x, vw[:, at : at + tile], preferred_element_type=F32) * scale
            p0[:, at : at + tile] = p[:count]
            if h == 0:
                tl[:, cols] = p[count : 2 * count].astype(BF16)
                pr[:, cols] = p[2 * count :]
            else:
                tr[:, cols] = p[2 * count :].astype(BF16)
                pl_[:, cols] = p[count : 2 * count]
    for copy in copies[3:7]:
        copy.wait()
    up_a = jnp.concatenate([vsa[...], vla[...], vrt[:, :half]], axis=0)
    up_b = jnp.concatenate([vsb[...], vlt[:, :half], vrb[...]], axis=0)
    for k in range(0, part, 256):
        g = times_turned(up_a, vw[k : k + 256, :half]) + times_turned(up_b, vw[k : k + 256, half:])
        g = (g * scale).astype(BF16)
        g0[:, k : k + 256] = g[:count]
        tl[:, half + k : half + k + 256] = g[count : 2 * count]
        tr[:, half + k : half + k + 256] = g[2 * count :]


def pass_kernel(pr, pl_, in_a, in_b, dr, dl):
    half = pr.shape[1]
    dr[:, :half] = (pr[...] + in_a[:, :half].astype(F32)).astype(BF16)
    dr[:, half:] = in_a[:, half:]
    dl[:, :half] = (pl_[...] + in_b[:, :half].astype(F32)).astype(BF16)
    dl[:, half:] = in_b[:, half:]


def result_kernel(n_x, me_ref, tok_ref, rstd_ref, p0, g0, lt, ld, rt, rd, out_p, out_x, back):
    me = me_ref[0]
    width, part = tok_ref.shape[1], g0.shape[1]
    rows = part // (width // part)
    half, quarter = width // 2, part // 2
    rstd = rstd_ref[:, :1]
    for h, (l, r) in enumerate(((ld, rt), (lt, rd))):
        cols = slice(h * half, (h + 1) * half)
        total = p0[:, cols] + l[:, :half].astype(F32) + r[:, :half].astype(F32)
        out_p[:, cols] = (total * rstd).astype(BF16)
    for d in range(n_x):
        slot = lax.rem(me + d, n_x) * rows
        for k in range(part // rows):
            at = k * rows
            if d == 0:
                block = g0[:, at : at + rows]
            elif d == 1:
                block = rt[:, half + at : half + at + rows]
            elif d == 3:
                block = lt[:, half + at : half + at + rows]
            elif at < quarter:
                block = ld[:, half + at : half + at + rows]
            else:
                block = rd[:, half + at - quarter : half + at - quarter + rows]
            back[:, pl.ds(pl.multiple_of(slot + k * n_x * rows, rows), rows)] = block.astype(F32)
    g = back[...]
    xhat = tok_ref[...].astype(F32) * rstd
    mean = jnp.mean(g * xhat, axis=1, keepdims=True)
    out_x[...] = (g - xhat * mean).astype(BF16)


def step_kernel(parts_ref, weight_ref, gain_ref, dep_1, dep_2, out_w_ref, out_g_ref):
    gain = gain_ref[...].astype(F32)
    grad = jnp.sum(parts_ref[...].astype(F32), axis=0)
    w = weight_ref[...].astype(F32)
    slope = jnp.sum(grad * w, axis=1, keepdims=True)
    out_w_ref[...] = (w - step_rate * (column_of(gain) * grad)).astype(BF16)
    out_g_ref[...] = (gain - gain_rate * row_of(slope)).astype(BF16)


def mean_kernel(w_ref, pw_ref, g_ref, pg_ref, out_w_ref, out_g_ref):
    out_w_ref[...] = (0.5 * (w_ref[...].astype(F32) + pw_ref[...].astype(F32))).astype(BF16)
    out_g_ref[...] = (0.5 * (g_ref[...].astype(F32) + pg_ref[...].astype(F32))).astype(BF16)


def on_device(tokens, weight, gain, upstream, step):
    n_x, n_y = lax.axis_size("x"), lax.axis_size("yh")
    rows, width_out = weight.shape
    count, width_in = tokens.shape
    scale = 1.0 / math.sqrt(width_in)
    half = width_out // 2
    part = n_y * rows
    me = jnp.stack([lax.axis_index("x"), lax.axis_index("yh")]).astype(jnp.int32)
    gain_row = gain.reshape(1, rows)
    flops = 2 * n_x * count * part * width_out
    moved = 2 * (n_x * count * (part + width_out) + part * width_out)
    quarter = part // 2
    vmem = lambda *shape: pltpu.VMEM(shape, BF16)
    sems = lambda n: pltpu.SemaphoreType.DMA((n,))
    short, long = (count, half + quarter), (count, half + part)

    (copies,) = call(
        weight_kernel,
        [(gain_row, BLOCK), (weight, BLOCK)],
        [in_hbm((n_y, rows, width_out))],
    )
    full_weight = exchange(copies, "yh").reshape(part, width_out)

    x_own, sa, sb, ta, tb, rstd = call(
        functools.partial(token_kernel, n_x),
        [(me, SCALAR), (tokens, HERE), (upstream, HERE), (copies, DEP)],
        [
            in_hbm((count, part)),
            in_hbm(short),
            in_hbm(short),
            array(long),
            array(long),
            in_hbm((count, 128), F32),
        ],
    )
    la, rb = shifted(sa, "x", 1), shifted(sb, "x", -1)
    lt, rt = shifted(ta, "x", 1), shifted(tb, "x", -1)
    fa, fb = shifted(la, "x", 1), shifted(rb, "x", -1)

    near = [(v, ANY) for v in (x_own, lt, rt, sa, la, sb, rb)]
    near_scratch = [vmem(count, part)] + [vmem(*long)] * 2 + [vmem(count, half)] * 4
    (near_w,) = call(
        grad_kernel,
        near,
        [array((part, width_out), F32)],
        near_scratch + [vmem(part, 3 * count), sems(7)],
        flops * 3 // 4,
        moved,
    )
    (part_w,) = call(
        functools.partial(grad_far_kernel, scale),
        [(near_w, HERE), (fa, HERE), (fb, HERE)],
        [(in_hbm((n_y, rows, width_out)),)],
        [vmem(part, count), vmem(2, n_y, rows, half), sems(2)],
        flops // 4,
        moved,
    )

    pieces_w = exchange(part_w, "yh")
    out_a, out_b = call(
        functools.partial(far_kernel, scale),
        [(fa, HERE), (fb, HERE), (full_weight, DEP)],
        [array(short), array(short)],
        [vmem(part, width_out), sems(2)],
        flops // 2,
        moved // 2,
    )
    in_a, in_b = shifted(out_a, "x", 1), shifted(out_b, "x", -1)
    p0, g0, tr, tl, pr, pl_ = call(
        functools.partial(near_kernel, scale),
        near + [(full_weight, DEP), (out_a, DEP)],
        [in_hbm((count, width_out), F32), in_hbm((count, part)), array(long), array(long)]
        + [array((count, half), F32)] * 2,
        near_scratch + [vmem(part, width_out), sems(9)],
        2 * flops,
        2 * moved,
    )
    got_lt, got_rt = shifted(tr, "x", 1), shifted(tl, "x", -1)
    dr, dl = call(
        pass_kernel,
        [(pr, HERE), (pl_, HERE), (in_a, HERE), (in_b, HERE)],
        [array(short), array(short)],
        moved=moved,
    )
    got_ld, got_rd = shifted(dr, "x", 1), shifted(dl, "x", -1)

    stepped = call(
        step_kernel,
        [(v, HERE) for v in (pieces_w, weight, gain_row)] + [(got_ld, DEP), (got_rd, DEP)],
        [array((rows, width_out)), array((1, rows))],
        moved=moved,
    )

    def gossip(distance):
        def branch(stepped, rest):
            peer = [shifted(v, "rep", distance) for v in stepped]
            results = call(
                functools.partial(result_kernel, n_x),
                [(rest[0], SCALAR)] + [(v, BLOCK) for v in rest[1:]],
                [in_hbm((count, width_out)), in_hbm((count, width_in))],
                [pltpu.VMEM((count, width_in), F32)],
                moved=moved,
            )
            means = call(
                mean_kernel,
                [(v, HERE) for v in (stepped[0], peer[0], stepped[1], peer[1])],
                [in_hbm((rows, width_out)), in_hbm((1, rows))],
            )
            return *results, *means

        return branch

    projected, input_gradient, new_weight, new_gain = lax.switch(
        step[0] % 4,
        [gossip(distance) for distance in (1, 2, 4, 8)],
        stepped,
        (me, tokens, rstd, p0, g0, got_lt, got_ld, got_rt, got_rd),
    )
    return projected, input_gradient, new_weight, new_gain.reshape(rows)


def solution(mesh):
    n_rep, n_fsdp = mesh.devices.shape
    n_x = 4
    split = Mesh(mesh.devices.reshape(n_rep, n_fsdp // n_x, n_x), ("rep", "yh", "x"))
    every = ("rep", "yh", "x")
    placed = (P(every, None), P(every, None), P(every), P(every, None), P())
    return jax.shard_map(
        on_device,
        mesh=split,
        in_specs=placed,
        out_specs=(P(every, None), P(every, None), P(every, None), P(every)),
        check_vma=False,
    )
```

```python
import functools
import math

import jax
import jax.numpy as jnp
from jax import lax
from jax.experimental import pallas as pl
from jax.experimental.pallas import tpu as pltpu
from jax.sharding import Mesh
from jax.sharding import PartitionSpec as P

eps = 1e-05
step_rate = 0.75
gain_rate = 0.004
F32 = jnp.float32
BF16 = jnp.bfloat16
VMEM_LIMIT = 32 * 1024 * 1024
ANY = pl.BlockSpec(memory_space=pl.ANY)
DEP = pl.BlockSpec(memory_space=pl.ANY)
BLOCK, AUTO = "block", "auto"
HERE = pl.BlockSpec(memory_space=pltpu.VMEM)
SCALAR = pl.BlockSpec(memory_space=pltpu.SMEM)


def array(shape, dtype=BF16):
    return jax.ShapeDtypeStruct(shape, dtype)


def in_hbm(shape, dtype=BF16):
    return pltpu.HBM(shape, dtype)


def call(kernel, ins, outs, scratch=(), flops=0, moved=0):
    values = [
        pltpu.with_memory_space_constraint(v, pltpu.HBM) if spec is ANY or spec is BLOCK else v
        for v, spec in ins
    ]

    def out_spec(shape):
        if isinstance(shape, tuple):
            return ANY
        return HERE if isinstance(shape, jax.ShapeDtypeStruct) else whole(shape.shape)

    return pl.pallas_call(
        kernel,
        grid=(1,),
        out_shape=[shape[0] if isinstance(shape, tuple) else shape for shape in outs],
        in_specs=[whole(v.shape) if spec in (BLOCK, AUTO) else spec for v, spec in ins],
        out_specs=[out_spec(shape) for shape in outs],
        scratch_shapes=list(scratch),
        compiler_params=pltpu.CompilerParams(vmem_limit_bytes=VMEM_LIMIT),
        cost_estimate=pl.CostEstimate(flops=flops, bytes_accessed=moved, transcendentals=0),
    )(*values)


def whole(shape):
    return pl.BlockSpec(shape, lambda s: (0,) * len(shape))


def fetch(pairs, sems):
    copies = [pltpu.make_async_copy(src, dst, sems.at[i]) for i, (src, dst) in enumerate(pairs)]
    for copy in copies:
        copy.start()
    return copies


def shifted(value, axis, steps):
    count = lax.axis_size(axis)
    pairs = [(source, (source + steps) % count) for source in range(count)]
    return lax.ppermute(value, axis, pairs)


def exchange(blocks, axis):
    return lax.all_to_all(blocks, axis, split_axis=0, concat_axis=0, tiled=True)


def column_of(row):
    n = row.shape[1]
    down = lax.broadcasted_iota(jnp.int32, (n, n), 0)
    along = lax.broadcasted_iota(jnp.int32, (n, n), 1)
    return jnp.sum(jnp.where(down == along, row, 0.0), axis=1, keepdims=True)


def row_of(column):
    n = column.shape[0]
    down = lax.broadcasted_iota(jnp.int32, (n, n), 0)
    along = lax.broadcasted_iota(jnp.int32, (n, n), 1)
    return jnp.sum(jnp.where(down == along, column, 0.0), axis=0, keepdims=True)


def weight_kernel(gain_ref, weight_ref, out_ref):
    scaled = (weight_ref[...].astype(F32) * column_of(gain_ref[...].astype(F32))).astype(BF16)
    for i in range(out_ref.shape[0]):
        out_ref[i] = scaled


def token_kernel(
    n_x, me_ref, vt, vu, dep, own_ref, sa_ref, sb_ref, ta_ref, tb_ref, rstd_ref
):
    me = me_ref[0]
    width, part = vt.shape[1], own_ref.shape[1]
    rows = part // (width // part)
    half, quarter = width // 2, part // 2
    for d in range(n_x):
        slot = lax.rem(me + d, n_x) * rows
        for k in range(part // rows):
            block = vt[:, pl.ds(pl.multiple_of(slot + k * n_x * rows, rows), rows)]
            at = k * rows
            if d == 0:
                own_ref[:, at : at + rows] = block
            elif d == 1:
                ta_ref[:, half + at : half + at + rows] = block
            elif d == 3:
                tb_ref[:, half + at : half + at + rows] = block
            elif at < quarter:
                sa_ref[:, half + at : half + at + rows] = block
            else:
                sb_ref[:, half + at - quarter : half + at - quarter + rows] = block
    x = vt[...].astype(F32)
    rstd = lax.rsqrt(jnp.mean(x * x, axis=1, keepdims=True) + eps)
    rstd_ref[...] = jnp.broadcast_to(rstd, rstd_ref.shape)
    up_a = (vu[:, :half].astype(F32) * rstd).astype(BF16)
    up_b = (vu[:, half:].astype(F32) * rstd).astype(BF16)
    sa_ref[:, :half] = up_a
    tb_ref[:, :half] = up_a
    sb_ref[:, :half] = up_b
    ta_ref[:, :half] = up_b


def grad_kernel(xo, lt, rt, sa, la, sb, rb, out, vx, vlt, vrt, vsa, vla, vsb, vrb, turned, sems):
    half = vsa.shape[1]
    tile = 256
    copies = fetch(
        [
            (xo, vx),
            (lt, vlt),
            (rt, vrt),
            (sa.at[:, :half], vsa),
            (la.at[:, :half], vla),
            (sb.at[:, :half], vsb),
            (rb.at[:, :half], vrb),
        ],
        sems,
    )
    for copy in copies[:3]:
        copy.wait()
    turned[...] = jnp.concatenate([vx[...], vlt[:, half:], vrt[:, half:]], axis=0).T
    for h, refs in enumerate(((vsa, vla, vrt), (vsb, vlt, vrb))):
        for copy in copies[3 + 2 * h : 5 + 2 * h]:
            copy.wait()

        @pl.loop(0, half // tile)
        def _(j):
            cols = pl.ds(pl.multiple_of(j * tile, tile), tile)
            block = jnp.concatenate([r[:, cols] for r in refs], axis=0)
            to = pl.ds(pl.multiple_of(h * half + j * tile, tile), tile)
            out[:, to] = jnp.dot(turned[...], block, preferred_element_type=F32)


def grad_far_kernel(scale, near, fa, fb, out, turned, total, sems):
    half = near.shape[1] // 2
    rows = out.shape[1]
    tile = 256
    turned[...] = jnp.concatenate([fa[:, half:], fb[:, half:]], axis=1).T
    copies = []
    for h, ref in enumerate((fa, fb)):

        @pl.loop(0, half // tile)
        def _(j):
            cols = pl.ds(pl.multiple_of(j * tile, tile), tile)
            to = pl.ds(pl.multiple_of(h * half + j * tile, tile), tile)
            part = near[:, to] + jnp.dot(turned[...], ref[:, cols], preferred_element_type=F32)
            part = (part * scale).astype(BF16)
            for k in range(out.shape[0]):
                total[h, k, :, cols] = part[k * rows : (k + 1) * rows]

        copy = pltpu.make_async_copy(
            total.at[h], out.at[:, :, h * half : (h + 1) * half], sems.at[h]
        )
        copy.start()
        copies.append(copy)
    for copy in copies:
        copy.wait()


def times_turned(left, right):
    return lax.dot_general(left, right, (((1,), (1,)), ((), ())), preferred_element_type=F32)


def far_kernel(scale, fa, fb, w, out_a, out_b, vw, sems):
    part, width = w.shape
    half, quarter = width // 2, part // 2
    pieces = [(w.at[:, i * half : (i + 1) * half], vw.at[:, i * half : (i + 1) * half]) for i in range(2)]
    copies = fetch(pieces, sems)
    x = jnp.concatenate([fa[:, half:], fb[:, half:]], axis=1)
    g = 0.0
    for h, (u, out) in enumerate(((fa, out_a), (fb, out_b))):
        copies[h].wait()
        block = vw[:, h * half : (h + 1) * half]
        out[:, :half] = (jnp.dot(x, block, preferred_element_type=F32) * scale).astype(BF16)
        g = g + times_turned(u[:, :half], block)
    g = (g * scale).astype(BF16)
    out_a[:, half:] = g[:, :quarter]
    out_b[:, half:] = g[:, quarter:]


def near_kernel(
    scale, xo, lt, rt, sa, la, sb, rb, w, dep, p0, g0, tr, tl, pr, pl_, vx, vlt, vrt, vsa, vla, vsb, vrb, vw, sems
):
    part = w.shape[0]
    count, half = vsa.shape
    tile = half // 2
    copies = fetch(
        [
            (xo, vx),
            (lt, vlt),
            (rt, vrt),
            (sa.at[:, :half], vsa),
            (la.at[:, :half], vla),
            (sb.at[:, :half], vsb),
            (rb.at[:, :half], vrb),
            (w.at[:, :half], vw.at[:, :half]),
            (w.at[:, half:], vw.at[:, half:]),
        ],
        sems,
    )
    for copy in copies[:3]:
        copy.wait()
    x = jnp.concatenate([vx[...], vlt[:, half:], vrt[:, half:]], axis=0)
    for h in range(2):
        copies[7 + h].wait()
        for t in range(2):
            at = h * half + t * tile
            cols = slice(t * tile, (t + 1) * tile)
            p = jnp.dot(x, vw[:, at : at + tile], preferred_element_type=F32) * scale
            p0[:, at : at + tile] = p[:count]
            if h == 0:
                tl[:, cols] = p[count : 2 * count].astype(BF16)
                pr[:, cols] = p[2 * count :]
            else:
                tr[:, cols] = p[2 * count :].astype(BF16)
                pl_[:, cols] = p[count : 2 * count]
    for copy in copies[3:7]:
        copy.wait()
    up_a = jnp.concatenate([vsa[...], vla[...], vrt[:, :half]], axis=0)
    up_b = jnp.concatenate([vsb[...], vlt[:, :half], vrb[...]], axis=0)
    for k in range(0, part, 256):
        g = times_turned(up_a, vw[k : k + 256, :half]) + times_turned(up_b, vw[k : k + 256, half:])
        g = (g * scale).astype(BF16)
        g0[:, k : k + 256] = g[:count]
        tl[:, half + k : half + k + 256] = g[count : 2 * count]
        tr[:, half + k : half + k + 256] = g[2 * count :]


def pass_kernel(pr, pl_, in_a, in_b, dr, dl):
    half = pr.shape[1]
    dr[:, :half] = (pr[...] + in_a[:, :half].astype(F32)).astype(BF16)
    dr[:, half:] = in_a[:, half:]
    dl[:, :half] = (pl_[...] + in_b[:, :half].astype(F32)).astype(BF16)
    dl[:, half:] = in_b[:, half:]


def result_kernel(n_x, me_ref, tok_ref, rstd_ref, p0, g0, lt, ld, rt, rd, out_p, out_x, back):
    me = me_ref[0]
    width, part = tok_ref.shape[1], g0.shape[1]
    rows = part // (width // part)
    half, quarter = width // 2, part // 2
    rstd = rstd_ref[:, :1]
    for h, (l, r) in enumerate(((ld, rt), (lt, rd))):
        cols = slice(h * half, (h + 1) * half)
        total = p0[:, cols] + l[:, :half].astype(F32) + r[:, :half].astype(F32)
        out_p[:, cols] = (total * rstd).astype(BF16)
    for d in range(n_x):
        slot = lax.rem(me + d, n_x) * rows
        for k in range(part // rows):
            at = k * rows
            if d == 0:
                block = g0[:, at : at + rows]
            elif d == 1:
                block = rt[:, half + at : half + at + rows]
            elif d == 3:
                block = lt[:, half + at : half + at + rows]
            elif at < quarter:
                block = ld[:, half + at : half + at + rows]
            else:
                block = rd[:, half + at - quarter : half + at - quarter + rows]
            back[:, pl.ds(pl.multiple_of(slot + k * n_x * rows, rows), rows)] = block.astype(F32)
    g = back[...]
    xhat = tok_ref[...].astype(F32) * rstd
    mean = jnp.mean(g * xhat, axis=1, keepdims=True)
    out_x[...] = (g - xhat * mean).astype(BF16)


def step_kernel(parts_ref, weight_ref, gain_ref, dep, out_w_ref, out_g_ref):
    gain = gain_ref[...].astype(F32)
    grad = jnp.sum(parts_ref[...].astype(F32), axis=0)
    w = weight_ref[...].astype(F32)
    slope = jnp.sum(grad * w, axis=1, keepdims=True)
    out_w_ref[...] = (w - step_rate * (column_of(gain) * grad)).astype(BF16)
    out_g_ref[...] = (gain - gain_rate * row_of(slope)).astype(BF16)


def mean_kernel(w_ref, pw_ref, g_ref, pg_ref, out_w_ref, out_g_ref):
    out_w_ref[...] = (0.5 * (w_ref[...].astype(F32) + pw_ref[...].astype(F32))).astype(BF16)
    out_g_ref[...] = (0.5 * (g_ref[...].astype(F32) + pg_ref[...].astype(F32))).astype(BF16)


def on_device(tokens, weight, gain, upstream, step):
    n_x, n_y = lax.axis_size("x"), lax.axis_size("yh")
    rows, width_out = weight.shape
    count, width_in = tokens.shape
    scale = 1.0 / math.sqrt(width_in)
    half = width_out // 2
    part = n_y * rows
    me = jnp.stack([lax.axis_index("x"), lax.axis_index("yh")]).astype(jnp.int32)
    gain_row = gain.reshape(1, rows)
    flops = 2 * n_x * count * part * width_out
    moved = 2 * (n_x * count * (part + width_out) + part * width_out)
    quarter = part // 2
    vmem = lambda *shape: pltpu.VMEM(shape, BF16)
    sems = lambda n: pltpu.SemaphoreType.DMA((n,))
    short, long = (count, half + quarter), (count, half + part)

    (copies,) = call(
        weight_kernel,
        [(gain_row, BLOCK), (weight, BLOCK)],
        [in_hbm((n_y, rows, width_out))],
    )
    full_weight = exchange(copies, "yh").reshape(part, width_out)

    x_own, sa, sb, ta, tb, rstd = call(
        functools.partial(token_kernel, n_x),
        [(me, SCALAR), (tokens, HERE), (upstream, HERE), (copies, DEP)],
        [
            in_hbm((count, part)),
            in_hbm(short),
            in_hbm(short),
            array(long),
            array(long),
            in_hbm((count, 128), F32),
        ],
    )
    la, rb = shifted(sa, "x", 1), shifted(sb, "x", -1)
    lt, rt = shifted(ta, "x", 1), shifted(tb, "x", -1)
    fa, fb = shifted(la, "x", 1), shifted(rb, "x", -1)

    near = [(v, ANY) for v in (x_own, lt, rt, sa, la, sb, rb)]
    near_scratch = [vmem(count, part)] + [vmem(*long)] * 2 + [vmem(count, half)] * 4
    (near_w,) = call(
        grad_kernel,
        near,
        [array((part, width_out), F32)],
        near_scratch + [vmem(part, 3 * count), sems(7)],
        flops * 3 // 4,
        moved,
    )
    (part_w,) = call(
        functools.partial(grad_far_kernel, scale),
        [(near_w, HERE), (fa, HERE), (fb, HERE)],
        [(in_hbm((n_y, rows, width_out)),)],
        [vmem(part, count), vmem(2, n_y, rows, half), sems(2)],
        flops // 4,
        moved,
    )

    pieces_w = exchange(part_w, "yh")
    out_a, out_b = call(
        functools.partial(far_kernel, scale),
        [(fa, HERE), (fb, HERE), (full_weight, DEP)],
        [array(short), array(short)],
        [vmem(part, width_out), sems(2)],
        flops // 2,
        moved // 2,
    )
    in_a, in_b = shifted(out_a, "x", 1), shifted(out_b, "x", -1)
    p0, g0, tr, tl, pr, pl_ = call(
        functools.partial(near_kernel, scale),
        near + [(full_weight, DEP), (out_a, DEP)],
        [in_hbm((count, width_out), F32), in_hbm((count, part)), array(long), array(long)]
        + [array((count, half), F32)] * 2,
        near_scratch + [vmem(part, width_out), sems(9)],
        2 * flops,
        2 * moved,
    )
    got_lt, got_rt = shifted(tr, "x", 1), shifted(tl, "x", -1)
    dr, dl = call(
        pass_kernel,
        [(pr, HERE), (pl_, HERE), (in_a, HERE), (in_b, HERE)],
        [array(short), array(short)],
        moved=moved,
    )
    got_ld, got_rd = shifted(dr, "x", 1), shifted(dl, "x", -1)

    stepped = call(
        step_kernel,
        [(v, HERE) for v in (pieces_w, weight, gain_row)] + [(dl, DEP)],
        [array((rows, width_out)), array((1, rows))],
        moved=moved,
    )

    def gossip(distance):
        def branch(stepped, rest):
            peer = [shifted(v, "rep", distance) for v in stepped]
            results = call(
                functools.partial(result_kernel, n_x),
                [(rest[0], SCALAR)] + [(v, BLOCK) for v in rest[1:]],
                [in_hbm((count, width_out)), in_hbm((count, width_in))],
                [pltpu.VMEM((count, width_in), F32)],
                moved=moved,
            )
            means = call(
                mean_kernel,
                [(v, HERE) for v in (stepped[0], peer[0], stepped[1], peer[1])],
                [in_hbm((rows, width_out)), in_hbm((1, rows))],
            )
            return *results, *means

        return branch

    projected, input_gradient, new_weight, new_gain = lax.switch(
        step[0] % 4,
        [gossip(distance) for distance in (1, 2, 4, 8)],
        stepped,
        (me, tokens, rstd, p0, g0, got_lt, got_ld, got_rt, got_rd),
    )
    return projected, input_gradient, new_weight, new_gain.reshape(rows)


def solution(mesh):
    n_rep, n_fsdp = mesh.devices.shape
    n_x = 4
    split = Mesh(mesh.devices.reshape(n_rep, n_fsdp // n_x, n_x), ("rep", "yh", "x"))
    every = ("rep", "yh", "x")
    placed = (P(every, None), P(every, None), P(every), P(every, None), P())
    return jax.shard_map(
        on_device,
        mesh=split,
        in_specs=placed,
        out_specs=(P(every, None), P(every, None), P(every, None), P(every)),
        check_vma=False,
    )
```
